512 devices in a mesh: fsdp: 32 (over x, y_lo, core), blk: 16 (over z, y_hi).
Axes of the slice: x: 4, y: 8 (y_hi: 2, y_lo: 4; y = y_hi * 4 + y_lo), z: 8, core: 2. Of those that a mesh axis runs over, the one named last changes fastest.
Arguments:
- gradient: float32 [28672, 8192], P('fsdp', 'blk'), may hold values from -120 to 120
- left_basis: bfloat16 [768, 28672], P('blk', 'fsdp'), may hold values from -0.03125 to 0.03125
- right_basis: bfloat16 [8192, 8192], P('blk', 'fsdp'), may hold values from -0.0625 to 0.0625
- moment: float32 [768, 8192], P('blk', 'fsdp'), may hold values from -6 to 6
- variance: float32 [768, 8192], P('blk', 'fsdp'), may hold values from 0.05 to 5
Outputs:
- update: float32 [28672, 8192], P('fsdp', 'blk')
- new_moment: float32 [768, 8192], P('blk', 'fsdp')
- new_variance: float32 [768, 8192], P('blk', 'fsdp')
The draws below stay inside these ranges and needn't reach their ends.
All inputs are finite; a program needn't handle non-finite values.
Results may differ from the reference program's by a relative error of at most 0.006.
Values may be sent and summed in bfloat16 or wider, within the bound.
No kernel may reach another device: no remote copies, remote signals or barrier semaphores. Data moves between devices by JAX's collectives and lax.ppermute only.
A program may use at most 64 MiB of HBM per device.

```python
import math
import jax
import jax.numpy as jnp
from jax import lax

ROWS = 28672
COLS = 8192
DIRS = 768


def draw_gradient(key, part):
    key = jax.random.fold_in(key, 11)
    key_row, key_col, key_main = jax.random.split(key, 3)
    row_u = jax.random.uniform(key_row, (ROWS, 1), jnp.float32)
    col_u = jax.random.uniform(key_col, (1, COLS), jnp.float32)
    row_pos = jnp.arange(ROWS, dtype=jnp.float32).reshape(ROWS, 1) / ROWS - 0.5
    col_pos = jnp.arange(COLS, dtype=jnp.float32).reshape(1, COLS) / COLS - 0.5
    rising = jnp.power(3.0, row_pos) * jnp.power(3.0, col_pos)
    spread = 10.0
    values = jnp.clip(jax.random.normal(key_main, (ROWS, COLS), jnp.float32), -6.0, 6.0)
    scales = jnp.power(spread, row_u - 0.5) * jnp.power(spread, col_u - 0.5) * rising
    return 0.6 * values * scales


def level_of(stream_key, extent, cuts, least, largest):
    def one(dim, blocks):
        steps = jax.random.uniform(jax.random.fold_in(jax.random.fold_in(stream_key, 6), dim), (blocks,), jnp.float32, least / len(cuts), largest / len(cuts))
        return jnp.repeat(jnp.exp(steps), extent[dim] // blocks).reshape((-1,) + (1,) * (len(extent) - dim - 1))

    loudness = one(*cuts[0])
    for cut in cuts[1:]:
        loudness = loudness * one(*cut)
    return loudness


def normal_values(own_key, dims, width, reach, cuts=(), kind=jnp.bfloat16):
    drawn = width * jax.random.normal(own_key, dims, jnp.float32)
    if cuts:
        drawn = drawn * level_of(own_key, dims, cuts, -0.22, 0.18)
    return jnp.clip(drawn, -reach, reach).astype(kind)


def setup_inputs(seed: int = 0) -> dict:
    key_of = jax.random.split(jax.random.key(seed), 6)
    return {
        "gradient": draw_gradient(jax.random.fold_in(key_of[5], 71), 0),
        "left_basis": normal_values(key_of[1], (DIRS, ROWS), ROWS ** -0.5, 0.03125, ((0, 16), (1, 32))),
        "right_basis": normal_values(key_of[2], (COLS, COLS), COLS ** -0.5, 0.0625, ((0, 16), (1, 32))),
        "moment": normal_values(key_of[3], (DIRS, COLS), 1.0, 6.0, ((0, 16), (1, 32)), jnp.float32),
        "variance": jnp.clip(jnp.exp(math.log(5.0) - 4.6051702 * jax.random.uniform(key_of[4], (DIRS, COLS), jnp.float32) ** level_of(key_of[4], (DIRS, COLS), ((0, 16), (1, 32)), -0.2, 0.2)), 0.05, 5.0),
    }


beta_first = 0.9
beta_second = 0.95
adam_eps = 1e-08
graft_eps = 1e-06

def reference(gradient, left_basis, right_basis, moment, variance):
    grad_b = gradient.astype(jnp.bfloat16)
    projected = jnp.dot(left_basis, grad_b, preferred_element_type=jnp.float32).astype(jnp.bfloat16)
    rotated = jnp.dot(projected, right_basis, preferred_element_type=jnp.float32)
    new_moment = beta_first * moment + (1.0 - beta_first) * rotated
    new_variance = beta_second * variance + (1.0 - beta_second) * rotated * rotated
    direction = (new_moment / (jnp.sqrt(new_variance) + adam_eps)).astype(jnp.bfloat16)
    returned = lax.dot_general(direction, right_basis, (((1,), (1,)), ((), ())), preferred_element_type=jnp.float32).astype(jnp.bfloat16)
    unscaled = lax.dot_general(left_basis, returned, (((0,), (0,)), ((), ())), preferred_element_type=jnp.float32)
    grad_sq = jnp.sum(gradient * gradient)
    unscaled_sq = jnp.sum(unscaled * unscaled)
    update = unscaled * (jnp.sqrt(grad_sq) / (jnp.sqrt(unscaled_sq) + graft_eps))
    return (update, new_moment, new_variance)
```

```python
import jax
import jax.numpy as jnp
from jax import lax
from jax.sharding import Mesh, PartitionSpec as P

beta_first = 0.9
beta_second = 0.95
adam_eps = 1e-08
graft_eps = 1e-06

F = ("x", "y", "c")
B = ("z", "h")
f32 = jnp.float32
bf16 = jnp.bfloat16


def spread(block, axes, count):
    copies = jnp.broadcast_to(block[None], (count,) + block.shape)
    got = lax.all_to_all(copies, axes, 0, 0, tiled=True)
    return got.reshape((count * block.shape[0],) + block.shape[1:])


def collect(parts, axes, count):
    parts = parts.astype(bf16).reshape((count, parts.shape[0] // count) + parts.shape[1:])
    return jnp.sum(lax.all_to_all(parts, axes, 0, 0, tiled=True).astype(f32), axis=0)


def collect_cores(parts):
    half = parts.shape[0] // 2
    core = lax.axis_index("c")
    low, high = parts[:half], parts[half:]
    mine = jnp.where(core == 0, low, high)
    other = jnp.where(core == 0, high, low).astype(bf16)
    return mine + lax.ppermute(other, "c", [(0, 1), (1, 0)]).astype(f32)


def body(gradient, left_basis, right_basis, moment, variance):
    grad_b = gradient.astype(bf16)
    panels = spread(left_basis, B, 16)
    partial_value = jnp.dot(panels, grad_b, preferred_element_type=f32)
    rows = collect(collect_cores(partial_value), ("x", "y"), 16).astype(bf16)
    projected = lax.all_gather(spread(rows, ("x", "y"), 16), "c", axis=0, tiled=True)
    rotated = collect(
        jnp.dot(projected, right_basis, preferred_element_type=f32), B, 16
    )
    new_moment = beta_first * moment + (1.0 - beta_first) * rotated
    new_variance = beta_second * variance + (1.0 - beta_second) * rotated * rotated
    direction = (new_moment / (jnp.sqrt(new_variance) + adam_eps)).astype(bf16)
    partial_back = lax.dot_general(
        spread(direction, B, 16),
        right_basis,
        (((1,), (1,)), ((), ())),
        preferred_element_type=f32,
    )
    back = collect(collect_cores(partial_back), ("x", "y"), 16).astype(bf16)
    returned = lax.all_gather(spread(back, ("x", "y"), 16), "c", axis=0, tiled=True)
    unscaled = lax.dot_general(
        panels, returned, (((0,), (0,)), ((), ())), preferred_element_type=f32
    )
    lane = lax.broadcasted_iota(jnp.int32, (512, 128), 1)
    sums = jnp.where(lane == 0, jnp.sum(gradient * gradient), jnp.sum(unscaled * unscaled))
    sums = jnp.sum(lax.all_to_all(sums, F + B, 0, 0, tiled=True), axis=0)
    update = unscaled * (jnp.sqrt(sums[0]) / (jnp.sqrt(sums[1]) + graft_eps))
    return (update, new_moment, new_variance)


def solution(mesh):
    fine = Mesh(mesh.devices.reshape(4, 4, 2, 8, 2), F + B)
    return jax.shard_map(
        body,
        mesh=fine,
        in_specs=(P(F, B), P(B, F), P(B, F), P(B, F), P(B, F)),
        out_specs=(P(F, B), P(B, F), P(B, F)),
        check_vma=False,
    )
```

```python
import jax
import jax.numpy as jnp
from jax import lax
from jax.sharding import Mesh, PartitionSpec as P

beta_first = 0.9
beta_second = 0.95
adam_eps = 1e-08
graft_eps = 1e-06

F = ("x", "y", "c")
B = ("z", "h")
PAIR = [(0, 1), (1, 0)]
f32 = jnp.float32
bf16 = jnp.bfloat16


def spread(block, axes, count):
    copies = jnp.broadcast_to(block[None], (count,) + block.shape)
    return lax.all_to_all(copies, axes, 0, 0, tiled=True)


def collect(parts, axes):
    got = lax.all_to_all(parts.astype(bf16), axes, 0, 0, tiled=True)
    terms = [got[i].astype(f32) for i in range(got.shape[0])]
    while len(terms) > 1:
        terms = [a + b for a, b in zip(terms[::2], terms[1::2])]
    return terms[0]


def collect_rows(low, high):
    core = lax.axis_index("c")
    mine = jnp.where(core == 0, low, high)
    other = jnp.where(core == 0, high, low).astype(bf16)
    half = mine + lax.ppermute(other, "c", PAIR).astype(f32)
    return collect(half.reshape(16, 24, half.shape[-1]), ("x", "y"))


def gather_rows(rows):
    half = spread(rows, ("x", "y"), 16).reshape(384, rows.shape[-1])
    return lax.all_gather(half, "c", axis=0, tiled=True)


def body(gradient, left_basis, right_basis, moment, variance):
    theirs = lax.ppermute(left_basis, "h", PAIR)
    moments = lax.ppermute(jnp.stack([moment, variance]), "h", PAIR)
    moment = jnp.concatenate([moment, moments[0]])
    variance = jnp.concatenate([variance, moments[1]])

    grad_b = gradient.astype(bf16)
    panels_own = spread(left_basis, "z", 8).reshape(384, 896)
    panels_other = spread(theirs, "z", 8).reshape(384, 896)
    projected = gather_rows(
        collect_rows(
            jnp.dot(panels_own, grad_b, preferred_element_type=f32),
            jnp.dot(panels_other, grad_b, preferred_element_type=f32),
        ).astype(bf16)
    )
    partial_rot = jnp.dot(projected, right_basis, preferred_element_type=f32).astype(bf16)
    partial_rot = partial_rot.reshape(2, 8, 48, 256).transpose(1, 0, 2, 3).reshape(8, 96, 256)
    rotated = collect(partial_rot, "z")
    partner = lax.ppermute(rotated, "h", PAIR)
    rotated = rotated + jnp.concatenate([partner[48:], partner[:48]])
    new_moment = beta_first * moment + (1.0 - beta_first) * rotated
    new_variance = beta_second * variance + (1.0 - beta_second) * rotated * rotated
    direction = (new_moment / (jnp.sqrt(new_variance) + adam_eps)).astype(bf16)
    directions = spread(direction, "z", 8).reshape(8, 2, 48, 256)
    directions = directions.transpose(1, 0, 2, 3).reshape(768, 256)
    partial_back = lax.dot_general(
        directions, right_basis, (((1,), (1,)), ((), ())), preferred_element_type=f32
    )
    returned = gather_rows(collect_rows(partial_back[:384], partial_back[384:]).astype(bf16))
    panels = jnp.concatenate([panels_own, panels_other])
    unscaled = lax.dot_general(
        panels, returned, (((0,), (0,)), ((), ())), preferred_element_type=f32
    )
    lane = lax.broadcasted_iota(jnp.int32, (1, 128), 1)
    sums = jnp.where(lane == 0, jnp.sum(gradient * gradient), jnp.sum(unscaled * unscaled))
    sums = jnp.sum(lax.all_gather(sums, "c"), axis=0)
    sums = jnp.sum(spread(sums, ("x", "y", "z", "h"), 256), axis=(0, 1))
    update = unscaled * (jnp.sqrt(sums[0]) / (jnp.sqrt(sums[1]) + graft_eps))
    return (update, new_moment[:48], new_variance[:48])


def solution(mesh):
    fine = Mesh(mesh.devices.reshape(4, 4, 2, 8, 2), F + B)
    return jax.shard_map(
        body,
        mesh=fine,
        in_specs=(P(F, B), P(B, F), P(B, F), P(B, F), P(B, F)),
        out_specs=(P(F, B), P(B, F), P(B, F)),
        check_vma=False,
    )
```

```python
import jax
import jax.numpy as jnp
from jax import lax
from jax.experimental import pallas as pl
from jax.experimental.pallas import tpu as pltpu
from jax.sharding import Mesh, PartitionSpec as P

beta_first = 0.9
beta_second = 0.95
adam_eps = 1e-08
graft_eps = 1e-06

F = ("x", "y", "c")
B = ("z", "h")
SWAP = [(0, 1), (1, 0)]
TURN = [(16 * i + j, 16 * j + i) for i in range(16) for j in range(16)]
STEP = 4
f32 = jnp.float32
bf16 = jnp.bfloat16


def rotate_kernel(rows_ref, basis_ref, out_ref):
    rows = rows_ref[...]
    for j in range(STEP):
        out_ref[j] = jnp.dot(rows, basis_ref[j], preferred_element_type=f32).astype(bf16)


def rotate(rows, basis):
    return pl.pallas_call(
        rotate_kernel,
        grid=(32 // STEP,),
        in_specs=[
            pl.BlockSpec((24, 512), lambda i: (0, 0)),
            pl.BlockSpec((STEP, 512, 256), lambda i: (i, 0, 0)),
        ],
        out_specs=pl.BlockSpec((STEP, 24, 256), lambda i: (i, 0, 0)),
        out_shape=jax.ShapeDtypeStruct((32, 24, 256), bf16),
        cost_estimate=pl.CostEstimate(
            flops=2 * 24 * 512 * 8192, bytes_accessed=2 * 512 * 8192, transcendentals=0
        ),
    )(rows, basis)


def back_kernel(direction_ref, basis_ref, out_ref, total_ref):
    step = pl.program_id(0)

    @pl.when(step == 0)
    def _():
        total_ref[...] = jnp.zeros_like(total_ref)

    total = total_ref[...]
    for j in range(STEP):
        total += lax.dot_general(
            direction_ref[j], basis_ref[j], (((1,), (1,)), ((), ())), preferred_element_type=f32
        )
    total_ref[...] = total

    @pl.when(step == pl.num_programs(0) - 1)
    def _():
        out_ref[...] = total_ref[...].astype(bf16)


def rotate_back(direction, basis):
    return pl.pallas_call(
        back_kernel,
        grid=(32 // STEP,),
        in_specs=[
            pl.BlockSpec((STEP, 24, 256), lambda i: (i, 0, 0)),
            pl.BlockSpec((STEP, 512, 256), lambda i: (i, 0, 0)),
        ],
        out_specs=pl.BlockSpec((24, 512), lambda i: (0, 0)),
        out_shape=jax.ShapeDtypeStruct((24, 512), bf16),
        scratch_shapes=[pltpu.VMEM((24, 512), f32)],
        cost_estimate=pl.CostEstimate(
            flops=2 * 24 * 512 * 8192, bytes_accessed=2 * 512 * 8192, transcendentals=0
        ),
    )(direction, basis)


def spread(block, axes, count):
    copies = jnp.broadcast_to(block[None], (count,) + block.shape)
    return lax.all_to_all(copies, axes, 0, 0, tiled=True)


def collect(parts, axes):
    got = lax.all_to_all(parts, axes, 0, 0, tiled=True)
    terms = [got[i].astype(f32) for i in range(got.shape[0])]
    while len(terms) > 1:
        terms = [a + b for a, b in zip(terms[::2], terms[1::2])]
    return terms[0]


def body(gradient, left_basis, right_basis, moment, variance):
    first = lax.axis_index("c") == 0

    def sort(mine, theirs):
        return jnp.where(first, mine, theirs), jnp.where(first, theirs, mine)

    basis = lax.all_gather(right_basis, F)

    moments = jnp.stack([moment, variance])
    keep, send = sort(moments[:, :24], moments[:, 24:])
    blocks = sort(keep, lax.ppermute(send, "c", SWAP))
    moments = lax.ppermute(jnp.stack(blocks, axis=1), ("x", "y", "z", "h"), TURN)

    grad_b = gradient.astype(bf16)
    panels = spread(lax.all_gather(left_basis, "h", tiled=True), "z", 8).reshape(768, 896)
    partial_value = jnp.dot(panels, grad_b, preferred_element_type=f32).reshape(16, 2, 24, 512)
    keep, send = sort(partial_value[:, 0], partial_value[:, 1])
    keep += lax.ppermute(send.astype(bf16), "c", SWAP).astype(f32)
    projected = collect(keep.astype(bf16), ("x", "y")).astype(bf16)

    rotated = rotate(projected, basis).reshape(16, 2, 24, 256)
    rotated = collect(rotated, B)
    new_moment = beta_first * moments[0] + (1.0 - beta_first) * rotated
    new_variance = beta_second * moments[1] + (1.0 - beta_second) * rotated * rotated
    direction = (new_moment / (jnp.sqrt(new_variance) + adam_eps)).astype(bf16)
    returned = rotate_back(spread(direction, B, 16).reshape(32, 24, 256), basis)

    half = spread(returned, ("x", "y"), 16)
    halves = sort(half, lax.ppermute(half, "c", SWAP))
    returned = jnp.stack(halves, axis=1).reshape(768, 512)
    unscaled = lax.dot_general(
        panels, returned, (((0,), (0,)), ((), ())), preferred_element_type=f32
    )
    lane = lax.broadcasted_iota(jnp.int32, (1, 128), 1)
    sums = jnp.where(lane == 0, jnp.sum(gradient * gradient), jnp.sum(unscaled * unscaled))
    sums = jnp.sum(lax.all_gather(sums, "c"), axis=0)
    sums = jnp.sum(spread(sums, ("x", "y", "z", "h"), 256), axis=(0, 1))
    update = unscaled * (jnp.sqrt(sums[0]) / (jnp.sqrt(sums[1]) + graft_eps))

    moments = lax.ppermute(jnp.stack([new_moment, new_variance]), ("x", "y", "z", "h"), TURN)
    keep, send = sort(moments[:, 0], moments[:, 1])
    moments = jnp.concatenate(sort(keep, lax.ppermute(send, "c", SWAP)), axis=1)
    return (update, moments[0], moments[1])


def solution(mesh):
    fine = Mesh(mesh.devices.reshape(4, 4, 2, 8, 2), F + B)
    return jax.shard_map(
        body,
        mesh=fine,
        in_specs=(P(F, B), P(B, F), P(B, F), P(B, F), P(B, F)),
        out_specs=(P(F, B), P(B, F), P(B, F)),
        check_vma=False,
    )
```

```python
import jax
import jax.numpy as jnp
from jax import lax
from jax.experimental import pallas as pl
from jax.experimental.pallas import tpu as pltpu
from jax.sharding import Mesh, PartitionSpec as P

beta_first = 0.9
beta_second = 0.95
adam_eps = 1e-08
graft_eps = 1e-06

F = ("x", "y", "c")
B = ("z", "h")
SWAP = [(0, 1), (1, 0)]
TURN = [(16 * i + j, 16 * j + i) for i in range(16) for j in range(16)]
f32 = jnp.float32
bf16 = jnp.bfloat16


def scale_kernel(sums_ref, unscaled_ref, update_ref, factor_ref):
    @pl.when(pl.program_id(0) == 0)
    def _():
        total = jnp.sum(sums_ref[...], axis=0)
        total = jnp.sum(total, axis=1, keepdims=True)
        root = jnp.sqrt(total)
        factor_ref[...] = jnp.broadcast_to(root[0:1] / (root[1:2] + graft_eps), factor_ref.shape)

    update_ref[...] = unscaled_ref[...] * factor_ref[...]


def scale(sums, unscaled):
    rows, columns = unscaled.shape
    return pl.pallas_call(
        scale_kernel,
        grid=(4,),
        in_specs=[
            pl.BlockSpec(sums.shape, lambda i: (0, 0, 0)),
            pl.BlockSpec((rows // 4, columns), lambda i: (i, 0)),
        ],
        out_specs=pl.BlockSpec((rows // 4, columns), lambda i: (i, 0)),
        out_shape=jax.ShapeDtypeStruct(unscaled.shape, f32),
        scratch_shapes=[pltpu.VMEM((1, columns), f32)],
        cost_estimate=pl.CostEstimate(
            flops=rows * columns, bytes_accessed=8 * rows * columns, transcendentals=0
        ),
    )(sums, unscaled)


def lanes(values):
    return jnp.sum(jnp.sum(values * values, axis=0).reshape(-1, 128), axis=0)


def spread(block, axes, count):
    copies = jnp.broadcast_to(block[None], (count,) + block.shape)
    return lax.all_to_all(copies, axes, 0, 0, tiled=True)


def collect(parts, axes):
    got = lax.all_to_all(parts, axes, 0, 0, tiled=True)
    terms = [got[i].astype(f32) for i in range(got.shape[0])]
    while len(terms) > 1:
        terms = [a + b for a, b in zip(terms[::2], terms[1::2])]
    return terms[0]


def body(gradient, left_basis, right_basis, moment, variance):
    first = lax.axis_index("c") == 0

    def sort(mine, theirs):
        return jnp.where(first, mine, theirs), jnp.where(first, theirs, mine)

    basis = lax.all_gather(right_basis, F)

    moments = jnp.stack([moment, variance])
    keep, send = sort(moments[:, :24], moments[:, 24:])
    blocks = sort(keep, lax.ppermute(send, "c", SWAP))
    moments = lax.ppermute(jnp.stack(blocks, axis=1), ("x", "y", "z", "h"), TURN)

    grad_b = gradient.astype(bf16)
    panels = spread(lax.all_gather(left_basis, "h", tiled=True), "z", 8)
    panels, moments, grad_lanes = lax.optimization_barrier((panels, moments, lanes(gradient)))
    panels = panels.reshape(768, 896)
    partial_value = jnp.dot(panels, grad_b, preferred_element_type=f32).reshape(16, 2, 24, 512)
    keep, send = sort(partial_value[:, 0], partial_value[:, 1])
    keep += lax.ppermute(send.astype(bf16), "c", SWAP).astype(f32)
    projected = collect(keep.astype(bf16), ("x", "y")).astype(bf16)

    rotated = jnp.einsum("rk,fkn->frn", projected, basis, preferred_element_type=f32)
    rotated = collect(rotated.astype(bf16).reshape(16, 2, 24, 256), B)
    new_moment = beta_first * moments[0] + (1.0 - beta_first) * rotated
    new_variance = beta_second * moments[1] + (1.0 - beta_second) * rotated * rotated
    direction = (new_moment / (jnp.sqrt(new_variance) + adam_eps)).astype(bf16)
    direction = spread(direction, B, 16).reshape(32, 24, 256)
    returned = lax.dot_general(
        direction, basis, (((0, 2), (0, 2)), ((), ())), preferred_element_type=f32
    )

    half = spread(returned.astype(bf16), ("x", "y"), 16)
    returned = lax.all_gather(half, "c", axis=1, tiled=True).reshape(768, 512)
    unscaled = lax.dot_general(
        panels, returned, (((0,), (0,)), ((), ())), preferred_element_type=f32
    )
    sums = jnp.stack([grad_lanes, lanes(unscaled)])
    sums = jnp.sum(lax.all_gather(sums, "c"), axis=0)
    update = scale(spread(sums, ("x", "y", "z", "h"), 256), unscaled)

    moments = lax.ppermute(jnp.stack([new_moment, new_variance]), ("x", "y", "z", "h"), TURN)
    keep, send = sort(moments[:, 0], moments[:, 1])
    moments = jnp.concatenate(sort(keep, lax.ppermute(send, "c", SWAP)), axis=1)
    return (update, moments[0], moments[1])


def solution(mesh):
    fine = Mesh(mesh.devices.reshape(4, 4, 2, 8, 2), F + B)
    return jax.shard_map(
        body,
        mesh=fine,
        in_specs=(P(F, B), P(B, F), P(B, F), P(B, F), P(B, F)),
        out_specs=(P(F, B), P(B, F), P(B, F)),
        check_vma=False,
    )
```

```python
import jax
import jax.numpy as jnp
from jax import lax
from jax.experimental import pallas as pl
from jax.experimental.pallas import tpu as pltpu
from jax.sharding import Mesh, PartitionSpec as P

beta_first = 0.9
beta_second = 0.95
adam_eps = 1e-08
graft_eps = 1e-06

F = ("x", "y", "c")
B = ("z", "h")
SWAP = [(0, 1), (1, 0)]
TURN = [(16 * i + j, 16 * j + i) for i in range(16) for j in range(16)]
f32 = jnp.float32
bf16 = jnp.bfloat16


def scale_kernel(sums_ref, unscaled_ref, update_ref, factor_ref):
    @pl.when(pl.program_id(0) == 0)
    def _():
        total = jnp.sum(sums_ref[...], axis=0)
        total = jnp.sum(total, axis=1, keepdims=True)
        root = jnp.sqrt(total)
        factor_ref[...] = jnp.broadcast_to(root[0:1] / (root[1:2] + graft_eps), factor_ref.shape)

    update_ref[...] = unscaled_ref[...] * factor_ref[...]


def scale(sums, unscaled):
    rows, columns = unscaled.shape
    return pl.pallas_call(
        scale_kernel,
        grid=(2,),
        in_specs=[
            pl.BlockSpec(sums.shape, lambda i: (0, 0, 0)),
            pl.BlockSpec((rows // 2, columns), lambda i: (i, 0)),
        ],
        out_specs=pl.BlockSpec((rows // 2, columns), lambda i: (i, 0)),
        out_shape=jax.ShapeDtypeStruct(unscaled.shape, f32),
        scratch_shapes=[pltpu.VMEM((1, columns), f32)],
        cost_estimate=pl.CostEstimate(
            flops=rows * columns, bytes_accessed=8 * rows * columns, transcendentals=0
        ),
    )(sums, unscaled)


def lanes(values):
    return jnp.sum(jnp.sum(values * values, axis=0).reshape(-1, 128), axis=0)


def adam(moment, variance, rotated):
    new_moment = beta_first * moment + (1.0 - beta_first) * rotated
    new_variance = beta_second * variance + (1.0 - beta_second) * rotated * rotated
    return new_moment, new_variance, new_moment / (jnp.sqrt(new_variance) + adam_eps)


def spread(block, axes, count):
    copies = jnp.broadcast_to(block[None], (count,) + block.shape)
    return lax.all_to_all(copies, axes, 0, 0, tiled=True)


def collect(parts, axes):
    got = lax.all_to_all(parts, axes, 0, 0, tiled=True)
    terms = [got[i].astype(f32) for i in range(got.shape[0])]
    while len(terms) > 1:
        terms = [a + b for a, b in zip(terms[::2], terms[1::2])]
    return terms[0]


def body(gradient, left_basis, right_basis, moment, variance):
    first = lax.axis_index("c") == 0

    def sort(mine, theirs):
        return jnp.where(first, mine, theirs), jnp.where(first, theirs, mine)

    basis = lax.all_gather(right_basis, F)

    moments = jnp.stack([moment, variance])
    keep, send = sort(moments[:, :24], moments[:, 24:])
    blocks = sort(keep, lax.ppermute(send, "c", SWAP))
    moments = jnp.stack(blocks, axis=1)

    grad_b = gradient.astype(bf16)
    panels = spread(lax.all_gather(left_basis, "h", tiled=True), "z", 8)
    panels, moments, grad_lanes = lax.optimization_barrier((panels, moments, lanes(gradient)))
    moments = lax.ppermute(moments, ("x", "y", "z", "h"), TURN)
    panels = panels.reshape(768, 896)
    partial_value = jnp.dot(panels, grad_b, preferred_element_type=f32).reshape(16, 2, 24, 512)
    keep, send = sort(partial_value[:, 0], partial_value[:, 1])
    keep += lax.ppermute(send.astype(bf16), "c", SWAP).astype(f32)
    projected = collect(keep.astype(bf16), ("x", "y")).astype(bf16)
    projected, moments = lax.optimization_barrier((projected, moments))

    rotated = jnp.einsum("rk,fkn->frn", projected, basis, preferred_element_type=f32)
    rotated = collect(rotated.astype(bf16).reshape(16, 2, 24, 256), B)
    direction = (adam(moments[0], moments[1], rotated)[2]).astype(bf16)
    direction = spread(direction, B, 16).reshape(32, 24, 256)
    returned = lax.dot_general(
        direction, basis, (((0, 2), (0, 2)), ((), ())), preferred_element_type=f32
    )

    half = spread(returned.astype(bf16), ("x", "y"), 16)
    returned = lax.all_gather(half, "c", axis=1, tiled=True).reshape(768, 512)
    unscaled = lax.dot_general(
        panels, returned, (((0,), (0,)), ((), ())), preferred_element_type=f32
    )
    sums = jnp.stack([grad_lanes, lanes(unscaled)])
    sums = jnp.sum(spread(sums, ("x", "c"), 8), axis=0)
    update = scale(spread(sums, ("y", "z", "h"), 64), unscaled)

    rotated = lax.ppermute(rotated, ("x", "y", "z", "h"), TURN)
    keep, send = sort(rotated[0], rotated[1])
    rotated = jnp.concatenate(sort(keep, lax.ppermute(send, "c", SWAP)))
    new_moment, new_variance, _ = adam(moment, variance, rotated)
    return (update, new_moment, new_variance)


def solution(mesh):
    fine = Mesh(mesh.devices.reshape(4, 4, 2, 8, 2), F + B)
    return jax.shard_map(
        body,
        mesh=fine,
        in_specs=(P(F, B), P(B, F), P(B, F), P(B, F), P(B, F)),
        out_specs=(P(F, B), P(B, F), P(B, F)),
        check_vma=False,
    )
```

```python
import jax
import jax.numpy as jnp
from jax import lax
from jax.experimental import pallas as pl
from jax.experimental.pallas import tpu as pltpu
from jax.sharding import Mesh, PartitionSpec as P

beta_first = 0.9
beta_second = 0.95
adam_eps = 1e-08
graft_eps = 1e-06

F = ("x", "y", "c")
B = ("z", "h")
SWAP = [(0, 1), (1, 0)]
TURN = [(16 * i + j, 16 * j + i) for i in range(16) for j in range(16)]
f32 = jnp.float32
bf16 = jnp.bfloat16


def scale_kernel(sums_ref, unscaled_ref, update_ref, factor_ref):
    @pl.when(pl.program_id(0) == 0)
    def _():
        total = jnp.sum(sums_ref[...], axis=0)
        total = jnp.sum(total, axis=1, keepdims=True)
        root = jnp.sqrt(total)
        factor_ref[...] = jnp.broadcast_to(root[0:1] / (root[1:2] + graft_eps), factor_ref.shape)

    update_ref[...] = unscaled_ref[...] * factor_ref[...]


def scale(sums, unscaled):
    rows, columns = unscaled.shape
    return pl.pallas_call(
        scale_kernel,
        grid=(2,),
        in_specs=[
            pl.BlockSpec(sums.shape, lambda i: (0, 0, 0)),
            pl.BlockSpec((rows // 2, columns), lambda i: (i, 0)),
        ],
        out_specs=pl.BlockSpec((rows // 2, columns), lambda i: (i, 0)),
        out_shape=jax.ShapeDtypeStruct(unscaled.shape, f32),
        scratch_shapes=[pltpu.VMEM((1, columns), f32)],
        cost_estimate=pl.CostEstimate(
            flops=rows * columns, bytes_accessed=8 * rows * columns, transcendentals=0
        ),
    )(sums, unscaled)


def lanes(values):
    return jnp.sum(jnp.sum(values * values, axis=0).reshape(-1, 128), axis=0)


def adam(moment, variance, rotated):
    new_moment = beta_first * moment + (1.0 - beta_first) * rotated
    new_variance = beta_second * variance + (1.0 - beta_second) * rotated * rotated
    return new_moment, new_variance, new_moment / (jnp.sqrt(new_variance) + adam_eps)


def spread(block, axes, count):
    copies = jnp.broadcast_to(block[None], (count,) + block.shape)
    return lax.all_to_all(copies, axes, 0, 0, tiled=True)


def collect(parts, axes):
    got = lax.all_to_all(parts, axes, 0, 0, tiled=True)
    terms = [got[i].astype(f32) for i in range(got.shape[0])]
    while len(terms) > 1:
        terms = [a + b for a, b in zip(terms[::2], terms[1::2])]
    return terms[0]


def body(gradient, left_basis, right_basis, moment, variance):
    first = lax.axis_index("c") == 0

    def sort(mine, theirs):
        return jnp.where(first, mine, theirs), jnp.where(first, theirs, mine)

    basis = lax.all_gather(right_basis, F)

    moments = jnp.stack([moment, variance])
    keep, send = sort(moments[:, :24], moments[:, 24:])
    blocks = sort(keep, lax.ppermute(send, "c", SWAP))
    moments = jnp.stack(blocks, axis=1)

    grad_b = gradient.astype(bf16)
    panels = spread(lax.all_gather(left_basis, "h", tiled=True), "z", 8)
    panels, moments, grad_lanes = lax.optimization_barrier((panels, moments, lanes(gradient)))
    moments = lax.ppermute(moments, ("x", "y", "z", "h"), TURN)
    panels = panels.reshape(768, 896)
    partial_value = jnp.dot(panels, grad_b, preferred_element_type=f32).reshape(16, 2, 24, 512)
    keep, send = sort(partial_value[:, 0], partial_value[:, 1])
    keep += lax.ppermute(send.astype(bf16), "c", SWAP).astype(f32)
    projected = collect(keep.astype(bf16), ("x", "y")).astype(bf16)
    projected, moments = lax.optimization_barrier((projected, moments))

    rotated = jnp.einsum("rk,fkn->frn", projected, basis, preferred_element_type=f32)
    rotated = collect(rotated.astype(bf16).reshape(16, 2, 24, 256), B)
    direction = (adam(moments[0], moments[1], rotated)[2]).astype(bf16)
    direction = spread(direction, B, 16).reshape(32, 24, 256)
    rotated = lax.ppermute(rotated, ("x", "y", "z", "h"), TURN)
    direction, rotated = lax.optimization_barrier((direction, rotated))
    returned = lax.dot_general(
        direction, basis, (((0, 2), (0, 2)), ((), ())), preferred_element_type=f32
    )

    half = spread(returned.astype(bf16), ("x", "y"), 16)
    keep, send = sort(rotated[0], rotated[1])
    rotated = jnp.concatenate(sort(keep, lax.ppermute(send, "c", SWAP)))
    new_moment, new_variance, _ = adam(moment, variance, rotated)
    half, new_moment, new_variance = lax.optimization_barrier((half, new_moment, new_variance))
    returned = lax.all_gather(half, "c", axis=1, tiled=True).reshape(768, 512)
    unscaled = lax.dot_general(
        panels, returned, (((0,), (0,)), ((), ())), preferred_element_type=f32
    )
    sums = jnp.stack([grad_lanes, lanes(unscaled)])
    sums = jnp.sum(spread(sums, ("x", "c"), 8), axis=0)
    update = scale(spread(sums, ("y", "z", "h"), 64), unscaled)
    return (update, new_moment, new_variance)


def solution(mesh):
    fine = Mesh(mesh.devices.reshape(4, 4, 2, 8, 2), F + B)
    return jax.shard_map(
        body,
        mesh=fine,
        in_specs=(P(F, B), P(B, F), P(B, F), P(B, F), P(B, F)),
        out_specs=(P(F, B), P(B, F), P(B, F)),
        check_vma=False,
    )
```

```python
import jax
import jax.numpy as jnp
from jax import lax
from jax.experimental import pallas as pl
from jax.experimental.pallas import tpu as pltpu
from jax.sharding import Mesh, PartitionSpec as P

beta_first = 0.9
beta_second = 0.95
adam_eps = 1e-08
graft_eps = 1e-06

F = ("x", "y", "c")
B = ("z", "h")
SWAP = [(0, 1), (1, 0)]
TURN = [(16 * i + j, 16 * j + i) for i in range(16) for j in range(16)]
f32 = jnp.float32
bf16 = jnp.bfloat16


def scale_kernel(sums_ref, unscaled_ref, update_ref, factor_ref):
    @pl.when(pl.program_id(0) == 0)
    def _():
        total = jnp.sum(sums_ref[...], axis=0)
        total = jnp.sum(total, axis=1, keepdims=True)
        root = jnp.sqrt(total)
        factor_ref[...] = jnp.broadcast_to(root[0:1] / (root[1:2] + graft_eps), factor_ref.shape)

    update_ref[...] = unscaled_ref[...] * factor_ref[...]


def scale(sums, unscaled):
    rows, columns = unscaled.shape
    return pl.pallas_call(
        scale_kernel,
        grid=(2,),
        in_specs=[
            pl.BlockSpec(sums.shape, lambda i: (0, 0, 0)),
            pl.BlockSpec((rows // 2, columns), lambda i: (i, 0)),
        ],
        out_specs=pl.BlockSpec((rows // 2, columns), lambda i: (i, 0)),
        out_shape=jax.ShapeDtypeStruct(unscaled.shape, f32),
        scratch_shapes=[pltpu.VMEM((1, columns), f32)],
        cost_estimate=pl.CostEstimate(
            flops=rows * columns, bytes_accessed=8 * rows * columns, transcendentals=0
        ),
    )(sums, unscaled)


def lanes(values):
    return jnp.sum(jnp.sum(values * values, axis=0).reshape(-1, 128), axis=0)


def adam(moment, variance, rotated):
    new_moment = beta_first * moment + (1.0 - beta_first) * rotated
    new_variance = beta_second * variance + (1.0 - beta_second) * rotated * rotated
    return new_moment, new_variance, new_moment / (jnp.sqrt(new_variance) + adam_eps)


def spread(block, axes, count):
    copies = jnp.broadcast_to(block[None], (count,) + block.shape)
    return lax.all_to_all(copies, axes, 0, 0, tiled=True)


def collect(parts, axes):
    got = lax.all_to_all(parts, axes, 0, 0, tiled=True)
    terms = [got[i].astype(f32) for i in range(got.shape[0])]
    while len(terms) > 1:
        terms = [a + b for a, b in zip(terms[::2], terms[1::2])]
    return terms[0]


def body(gradient, left_basis, right_basis, moment, variance):
    first = lax.axis_index("c") == 0

    def sort(mine, theirs):
        return jnp.where(first, mine, theirs), jnp.where(first, theirs, mine)

    basis = lax.all_gather(right_basis, F)

    moments = jnp.stack([moment, variance])
    keep, send = sort(moments[:, :24], moments[:, 24:])
    blocks = sort(keep, lax.ppermute(send, "c", SWAP))
    moments = jnp.stack(blocks, axis=1)

    grad_b = gradient.astype(bf16)
    panels = spread(lax.all_gather(left_basis, "h", tiled=True), "z", 8)
    panels, moments, grad_lanes = lax.optimization_barrier((panels, moments, lanes(gradient)))
    moments = lax.ppermute(moments, ("x", "y", "z", "h"), TURN)
    panels = panels.reshape(768, 896)
    partial_value = jnp.dot(panels, grad_b, preferred_element_type=f32).reshape(16, 2, 24, 512)
    keep, send = sort(partial_value[:, 0], partial_value[:, 1])
    keep += lax.ppermute(send.astype(bf16), "c", SWAP).astype(f32)
    projected = collect(keep.astype(bf16), ("x", "y")).astype(bf16)
    projected, moments = lax.optimization_barrier((projected, moments))

    rotated = jnp.einsum("rk,fkn->frn", projected, basis, preferred_element_type=f32)
    rotated = collect(rotated.astype(bf16).reshape(16, 2, 24, 256), B)
    direction = (adam(moments[0], moments[1], rotated)[2]).astype(bf16)
    direction = spread(direction, B, 16).reshape(32, 24, 256)
    returned = lax.dot_general(
        direction, basis, (((0, 2), (0, 2)), ((), ())), preferred_element_type=f32
    )

    half = spread(returned.astype(bf16), ("x", "y"), 16)
    keep, send = sort(rotated[0], rotated[1])
    rotated = jnp.concatenate(sort(keep, lax.ppermute(send, "c", SWAP)))
    half, rotated = lax.optimization_barrier((half, rotated))
    returned = lax.all_gather(half, "c", axis=1, tiled=True).reshape(768, 512)
    unscaled = lax.dot_general(
        panels, returned, (((0,), (0,)), ((), ())), preferred_element_type=f32
    )
    sums = jnp.stack([grad_lanes, lanes(unscaled)])
    sums = jnp.sum(spread(sums, ("x", "c"), 8), axis=0)
    sums, rotated = lax.optimization_barrier((sums, rotated))
    update = scale(spread(sums, ("y", "z", "h"), 64), unscaled)
    rotated = lax.ppermute(rotated, ("x", "y", "z", "h"), TURN)
    new_moment, new_variance, _ = adam(moment, variance, rotated)
    return (update, new_moment, new_variance)


def solution(mesh):
    fine = Mesh(mesh.devices.reshape(4, 4, 2, 8, 2), F + B)
    return jax.shard_map(
        body,
        mesh=fine,
        in_specs=(P(F, B), P(B, F), P(B, F), P(B, F), P(B, F)),
        out_specs=(P(F, B), P(B, F), P(B, F)),
        check_vma=False,
    )
```

```python
import jax
import jax.numpy as jnp
from jax import lax
from jax.experimental import pallas as pl
from jax.experimental.pallas import tpu as pltpu
from jax.sharding import Mesh, PartitionSpec as P

beta_first = 0.9
beta_second = 0.95
adam_eps = 1e-08
graft_eps = 1e-06

F = ("x", "y", "c")
B = ("z", "h")
SWAP = [(0, 1), (1, 0)]
TURN = [(16 * i + j, 16 * j + i) for i in range(16) for j in range(16)]
PARTS = 4
f32 = jnp.float32
bf16 = jnp.bfloat16


def scale_kernel(sums_ref, unscaled_ref, update_ref, scaled_ref, done_ref):
    total = jnp.sum(sums_ref[...], axis=0)
    root = jnp.sqrt(jnp.sum(total, axis=1, keepdims=True))
    factor = root[0:1] / (root[1:2] + graft_eps)
    size = scaled_ref.shape[0] // PARTS
    copies = []
    for part in range(PARTS):
        rows = pl.ds(part * size, size)
        scaled_ref[rows] = unscaled_ref[rows] * factor
        copies.append(
            pltpu.make_async_copy(scaled_ref.at[rows], update_ref.at[rows], done_ref.at[part])
        )
        copies[-1].start()
    for copy in copies:
        copy.wait()


def scale(sums, unscaled):
    return pl.pallas_call(
        scale_kernel,
        in_specs=[pl.BlockSpec(memory_space=pltpu.VMEM)] * 2,
        out_specs=pl.BlockSpec(memory_space=pl.ANY),
        out_shape=jax.ShapeDtypeStruct(unscaled.shape, f32),
        scratch_shapes=[
            pltpu.VMEM(unscaled.shape, f32),
            pltpu.SemaphoreType.DMA((PARTS,)),
        ],
        compiler_params=pltpu.CompilerParams(vmem_limit_bytes=16 * 2**20),
        cost_estimate=pl.CostEstimate(
            flops=unscaled.size, bytes_accessed=8 * unscaled.size, transcendentals=0
        ),
    )(sums, unscaled)


def lanes(values):
    return jnp.sum(jnp.sum(values * values, axis=0).reshape(-1, 128), axis=0)


def adam(moment, variance, rotated):
    new_moment = beta_first * moment + (1.0 - beta_first) * rotated
    new_variance = beta_second * variance + (1.0 - beta_second) * rotated * rotated
    return new_moment, new_variance, new_moment / (jnp.sqrt(new_variance) + adam_eps)


def spread(block, axes, count):
    copies = jnp.broadcast_to(block[None], (count,) + block.shape)
    return lax.all_to_all(copies, axes, 0, 0, tiled=True)


def collect(parts, axes):
    got = lax.all_to_all(parts, axes, 0, 0, tiled=True)
    terms = [got[i].astype(f32) for i in range(got.shape[0])]
    while len(terms) > 1:
        terms = [a + b for a, b in zip(terms[::2], terms[1::2])]
    return terms[0]


def body(gradient, left_basis, right_basis, moment, variance):
    first = lax.axis_index("c") == 0

    def sort(mine, theirs):
        return jnp.where(first, mine, theirs), jnp.where(first, theirs, mine)

    basis = lax.all_gather(right_basis, F)

    moments = jnp.stack([moment, variance])
    keep, send = sort(moments[:, :24], moments[:, 24:])
    blocks = sort(keep, lax.ppermute(send, "c", SWAP))
    moments = jnp.stack(blocks, axis=1)

    grad_b = gradient.astype(bf16)
    panels = spread(lax.all_gather(left_basis, "h", tiled=True), "z", 8)
    panels, moments, grad_lanes = lax.optimization_barrier((panels, moments, lanes(gradient)))
    moments = lax.ppermute(moments, ("x", "y", "z", "h"), TURN)
    panels = panels.reshape(768, 896)
    partial_value = jnp.dot(panels, grad_b, preferred_element_type=f32).reshape(16, 2, 24, 512)
    keep, send = sort(partial_value[:, 0], partial_value[:, 1])
    keep += lax.ppermute(send.astype(bf16), "c", SWAP).astype(f32)
    projected = collect(keep.astype(bf16), ("x", "y")).astype(bf16)
    projected, moments = lax.optimization_barrier((projected, moments))

    rotated = jnp.einsum("rk,fkn->frn", projected, basis, preferred_element_type=f32)
    rotated = collect(rotated.astype(bf16).reshape(16, 2, 24, 256), B)
    direction = (adam(moments[0], moments[1], rotated)[2]).astype(bf16)
    direction = spread(direction, B, 16).reshape(32, 24, 256)
    returned = lax.dot_general(
        direction, basis, (((0, 2), (0, 2)), ((), ())), preferred_element_type=f32
    )

    half = spread(returned.astype(bf16), ("x", "y"), 16)
    rotated = lax.ppermute(rotated, ("x", "y", "z", "h"), TURN)
    keep, send = sort(rotated[0], rotated[1])
    rotated = jnp.concatenate(sort(keep, lax.ppermute(send, "c", SWAP)))
    new_moment, new_variance, _ = adam(moment, variance, rotated)
    half, new_moment, new_variance = lax.optimization_barrier((half, new_moment, new_variance))
    returned = lax.all_gather(half, "c", axis=1, tiled=True).reshape(768, 512)
    unscaled = lax.dot_general(
        panels, returned, (((0,), (0,)), ((), ())), preferred_element_type=f32
    )
    sums = jnp.stack([grad_lanes, lanes(unscaled)])
    sums = jnp.sum(spread(sums, ("x", "c"), 8), axis=0)
    update = scale(spread(sums, ("y", "z", "h"), 64), unscaled)
    return (update, new_moment, new_variance)


def solution(mesh):
    fine = Mesh(mesh.devices.reshape(4, 4, 2, 8, 2), F + B)
    return jax.shard_map(
        body,
        mesh=fine,
        in_specs=(P(F, B), P(B, F), P(B, F), P(B, F), P(B, F)),
        out_specs=(P(F, B), P(B, F), P(B, F)),
        check_vma=False,
    )
```

```python
import jax
import jax.numpy as jnp
from jax import lax
from jax.experimental import pallas as pl
from jax.experimental.pallas import tpu as pltpu
from jax.sharding import Mesh, PartitionSpec as P

beta_first = 0.9
beta_second = 0.95
adam_eps = 1e-08
graft_eps = 1e-06

F = ("x", "y", "c")
B = ("z", "h")
SWAP = [(0, 1), (1, 0)]
TURN = [(16 * i + j, 16 * j + i) for i in range(16) for j in range(16)]
PARTS = 4
PIECES = 8
f32 = jnp.float32
bf16 = jnp.bfloat16


def fetch(basis_ref, held_ref, landed_ref):
    size = held_ref.shape[0] // PIECES
    copies = []
    for piece in range(PIECES):
        blocks = pl.ds(piece * size, size)
        copies.append(
            pltpu.make_async_copy(basis_ref.at[blocks], held_ref.at[blocks], landed_ref.at[piece])
        )
        copies[-1].start()
    return copies, size


def rotate_kernel(rows_ref, basis_ref, out_ref, held_ref, landed_ref):
    copies, size = fetch(basis_ref, held_ref, landed_ref)
    rows = rows_ref[...]
    for piece, copy in enumerate(copies):
        copy.wait()
        for block in range(piece * size, (piece + 1) * size):
            product = jnp.dot(rows, held_ref[block], preferred_element_type=f32)
            out_ref[block] = product.astype(bf16)


def back_kernel(direction_ref, basis_ref, out_ref, held_ref, landed_ref):
    copies, size = fetch(basis_ref, held_ref, landed_ref)
    total = jnp.zeros(out_ref.shape[1:], f32)
    for piece, copy in enumerate(copies):
        copy.wait()
        for block in range(piece * size, (piece + 1) * size):
            total += lax.dot_general(
                direction_ref[block],
                held_ref[block],
                (((1,), (1,)), ((), ())),
                preferred_element_type=f32,
            )
    total = total.astype(bf16)
    for target in range(out_ref.shape[0]):
        out_ref[target] = total


def with_basis(kernel, left, basis, shape):
    return pl.pallas_call(
        kernel,
        in_specs=[pl.BlockSpec(memory_space=pltpu.VMEM), pl.BlockSpec(memory_space=pl.ANY)],
        out_specs=pl.BlockSpec(memory_space=pltpu.VMEM),
        out_shape=jax.ShapeDtypeStruct(shape, bf16),
        scratch_shapes=[pltpu.VMEM(basis.shape, bf16), pltpu.SemaphoreType.DMA((PIECES,))],
        compiler_params=pltpu.CompilerParams(vmem_limit_bytes=24 * 2**20),
        cost_estimate=pl.CostEstimate(
            flops=48 * basis.size, bytes_accessed=2 * basis.size, transcendentals=0
        ),
    )(left, basis)


def scale_kernel(sums_ref, unscaled_ref, update_ref, scaled_ref, done_ref):
    total = jnp.sum(sums_ref[...], axis=0)
    root = jnp.sqrt(jnp.sum(total, axis=1, keepdims=True))
    factor = root[0:1] / (root[1:2] + graft_eps)
    size = scaled_ref.shape[0] // PARTS
    copies = []
    for part in range(PARTS):
        rows = pl.ds(part * size, size)
        scaled_ref[rows] = unscaled_ref[rows] * factor
        copies.append(
            pltpu.make_async_copy(scaled_ref.at[rows], update_ref.at[rows], done_ref.at[part])
        )
        copies[-1].start()
    for copy in copies:
        copy.wait()


def scale(sums, unscaled):
    return pl.pallas_call(
        scale_kernel,
        in_specs=[pl.BlockSpec(memory_space=pltpu.VMEM)] * 2,
        out_specs=pl.BlockSpec(memory_space=pl.ANY),
        out_shape=jax.ShapeDtypeStruct(unscaled.shape, f32),
        scratch_shapes=[
            pltpu.VMEM(unscaled.shape, f32),
            pltpu.SemaphoreType.DMA((PARTS,)),
        ],
        compiler_params=pltpu.CompilerParams(vmem_limit_bytes=16 * 2**20),
        cost_estimate=pl.CostEstimate(
            flops=unscaled.size, bytes_accessed=8 * unscaled.size, transcendentals=0
        ),
    )(sums, unscaled)


def lanes(values):
    return jnp.sum(jnp.sum(values * values, axis=0).reshape(-1, 128), axis=0)


def adam(moment, variance, rotated):
    new_moment = beta_first * moment + (1.0 - beta_first) * rotated
    new_variance = beta_second * variance + (1.0 - beta_second) * rotated * rotated
    return new_moment, new_variance, new_moment / (jnp.sqrt(new_variance) + adam_eps)


def spread(block, axes, count):
    copies = jnp.broadcast_to(block[None], (count,) + block.shape)
    return lax.all_to_all(copies, axes, 0, 0, tiled=True)


def collect(parts, axes):
    got = lax.all_to_all(parts, axes, 0, 0, tiled=True)
    terms = [got[i].astype(f32) for i in range(got.shape[0])]
    while len(terms) > 1:
        terms = [a + b for a, b in zip(terms[::2], terms[1::2])]
    return terms[0]


def body(gradient, left_basis, right_basis, moment, variance):
    first = lax.axis_index("c") == 0

    def sort(mine, theirs):
        return jnp.where(first, mine, theirs), jnp.where(first, theirs, mine)

    basis = lax.all_gather(right_basis, F)

    moments = jnp.stack([moment, variance])
    keep, send = sort(moments[:, :24], moments[:, 24:])
    blocks = sort(keep, lax.ppermute(send, "c", SWAP))
    moments = jnp.stack(blocks, axis=1)

    grad_b = gradient.astype(bf16)
    panels = spread(lax.all_gather(left_basis, "h", tiled=True), "z", 8)
    panels, moments, grad_lanes = lax.optimization_barrier((panels, moments, lanes(gradient)))
    moments = lax.ppermute(moments, ("x", "y", "z", "h"), TURN)
    panels = panels.reshape(768, 896)
    partial_value = jnp.dot(panels, grad_b, preferred_element_type=f32).reshape(16, 2, 24, 512)
    keep, send = sort(partial_value[:, 0], partial_value[:, 1])
    keep += lax.ppermute(send.astype(bf16), "c", SWAP).astype(f32)
    projected = collect(keep.astype(bf16), ("x", "y")).astype(bf16)
    projected, moments = lax.optimization_barrier((projected, moments))

    rotated = with_basis(rotate_kernel, projected, basis, (32, 24, 256))
    rotated = collect(rotated.reshape(16, 2, 24, 256), B)
    direction = (adam(moments[0], moments[1], rotated)[2]).astype(bf16)
    direction = spread(direction, B, 16).reshape(32, 24, 256)
    returned = with_basis(back_kernel, direction, basis, (16, 24, 512))
    half = lax.all_to_all(returned, ("x", "y"), 0, 0, tiled=True)
    rotated = lax.ppermute(rotated, ("x", "y", "z", "h"), TURN)
    keep, send = sort(rotated[0], rotated[1])
    rotated = jnp.concatenate(sort(keep, lax.ppermute(send, "c", SWAP)))
    new_moment, new_variance, _ = adam(moment, variance, rotated)
    half, new_moment, new_variance = lax.optimization_barrier((half, new_moment, new_variance))
    returned = lax.all_gather(half, "c", axis=1, tiled=True).reshape(768, 512)
    unscaled = lax.dot_general(
        panels, returned, (((0,), (0,)), ((), ())), preferred_element_type=f32
    )
    sums = jnp.stack([grad_lanes, lanes(unscaled)])
    sums = jnp.sum(spread(sums, ("x", "c"), 8), axis=0)
    update = scale(spread(sums, ("y", "z", "h"), 64), unscaled)
    return (update, new_moment, new_variance)


def solution(mesh):
    fine = Mesh(mesh.devices.reshape(4, 4, 2, 8, 2), F + B)
    return jax.shard_map(
        body,
        mesh=fine,
        in_specs=(P(F, B), P(B, F), P(B, F), P(B, F), P(B, F)),
        out_specs=(P(F, B), P(B, F), P(B, F)),
        check_vma=False,
    )
```

```python
import jax
import jax.numpy as jnp
from jax import lax
from jax.experimental import pallas as pl
from jax.experimental.pallas import tpu as pltpu
from jax.sharding import Mesh, PartitionSpec as P

beta_first = 0.9
beta_second = 0.95
adam_eps = 1e-08
graft_eps = 1e-06

F = ("x", "y", "c")
B = ("z", "h")
SWAP = [(0, 1), (1, 0)]
TURN = [(16 * i + j, 16 * j + i) for i in range(16) for j in range(16)]
PARTS = 4
PIECES = 8
f32 = jnp.float32
bf16 = jnp.bfloat16


def fetch(basis_ref, held_ref, landed_ref):
    size = held_ref.shape[0] // PIECES
    copies = []
    for piece in range(PIECES):
        blocks = pl.ds(piece * size, size)
        copies.append(
            pltpu.make_async_copy(basis_ref.at[blocks], held_ref.at[blocks], landed_ref.at[piece])
        )
        copies[-1].start()
    return copies, size


def rotate_kernel(rows_ref, basis_ref, out_ref, held_ref, landed_ref):
    copies, size = fetch(basis_ref, held_ref, landed_ref)
    rows = rows_ref[...]
    for piece, copy in enumerate(copies):
        copy.wait()
        for block in range(piece * size, (piece + 1) * size):
            product = jnp.dot(rows, held_ref[block], preferred_element_type=f32)
            out_ref[block] = product.astype(bf16)


def back_kernel(direction_ref, basis_ref, out_ref, held_ref, landed_ref):
    copies, size = fetch(basis_ref, held_ref, landed_ref)
    total = jnp.zeros(out_ref.shape[1:], f32)
    for piece, copy in enumerate(copies):
        copy.wait()
        for block in range(piece * size, (piece + 1) * size):
            total += lax.dot_general(
                direction_ref[block],
                held_ref[block],
                (((1,), (1,)), ((), ())),
                preferred_element_type=f32,
            )
    total = total.astype(bf16)
    for target in range(out_ref.shape[0]):
        out_ref[target] = total


def with_basis(kernel, left, basis, shape):
    return pl.pallas_call(
        kernel,
        in_specs=[pl.BlockSpec(memory_space=pltpu.VMEM), pl.BlockSpec(memory_space=pl.ANY)],
        out_specs=pl.BlockSpec(memory_space=pltpu.VMEM),
        out_shape=jax.ShapeDtypeStruct(shape, bf16),
        scratch_shapes=[pltpu.VMEM(basis.shape, bf16), pltpu.SemaphoreType.DMA((PIECES,))],
        compiler_params=pltpu.CompilerParams(vmem_limit_bytes=57 * 2**20),
        cost_estimate=pl.CostEstimate(
            flops=48 * basis.size, bytes_accessed=2 * basis.size, transcendentals=0
        ),
    )(left, basis)


def scale_kernel(sums_ref, unscaled_ref, update_ref, scaled_ref, done_ref):
    total = jnp.sum(sums_ref[...], axis=0)
    root = jnp.sqrt(jnp.sum(total, axis=1, keepdims=True))
    factor = root[0:1] / (root[1:2] + graft_eps)
    size = scaled_ref.shape[0] // PARTS
    copies = []
    for part in range(PARTS):
        rows = pl.ds(part * size, size)
        scaled_ref[rows] = unscaled_ref[rows] * factor
        copies.append(
            pltpu.make_async_copy(scaled_ref.at[rows], update_ref.at[rows], done_ref.at[part])
        )
        copies[-1].start()
    for copy in copies:
        copy.wait()


def scale(sums, unscaled):
    return pl.pallas_call(
        scale_kernel,
        in_specs=[pl.BlockSpec(memory_space=pltpu.VMEM)] * 2,
        out_specs=pl.BlockSpec(memory_space=pl.ANY),
        out_shape=jax.ShapeDtypeStruct(unscaled.shape, f32),
        scratch_shapes=[
            pltpu.VMEM(unscaled.shape, f32),
            pltpu.SemaphoreType.DMA((PARTS,)),
        ],
        compiler_params=pltpu.CompilerParams(vmem_limit_bytes=16 * 2**20),
        cost_estimate=pl.CostEstimate(
            flops=unscaled.size, bytes_accessed=8 * unscaled.size, transcendentals=0
        ),
    )(sums, unscaled)


def lanes(values):
    return jnp.sum(jnp.sum(values * values, axis=0).reshape(-1, 128), axis=0)


def adam(moment, variance, rotated):
    new_moment = beta_first * moment + (1.0 - beta_first) * rotated
    new_variance = beta_second * variance + (1.0 - beta_second) * rotated * rotated
    return new_moment, new_variance, new_moment / (jnp.sqrt(new_variance) + adam_eps)


def spread(block, axes, count):
    copies = jnp.broadcast_to(block[None], (count,) + block.shape)
    return lax.all_to_all(copies, axes, 0, 0, tiled=True)


def collect(parts, axes):
    got = lax.all_to_all(parts, axes, 0, 0, tiled=True)
    terms = [got[i].astype(f32) for i in range(got.shape[0])]
    while len(terms) > 1:
        terms = [a + b for a, b in zip(terms[::2], terms[1::2])]
    return terms[0]


def body(gradient, left_basis, right_basis, moment, variance):
    first = lax.axis_index("c") == 0

    def sort(mine, theirs):
        return jnp.where(first, mine, theirs), jnp.where(first, theirs, mine)

    basis = lax.all_gather(right_basis, F)

    moments = jnp.stack([moment, variance])
    keep, send = sort(moments[:, :24], moments[:, 24:])
    blocks = sort(keep, lax.ppermute(send, "c", SWAP))
    moments = jnp.stack(blocks, axis=1)

    grad_b = gradient.astype(bf16)
    panels = spread(lax.all_gather(left_basis, "h", tiled=True), "z", 8)
    panels, moments, grad_lanes = lax.optimization_barrier((panels, moments, lanes(gradient)))
    moments = lax.ppermute(moments, ("x", "y", "z", "h"), TURN)
    panels = panels.reshape(768, 896)
    partial_value = jnp.dot(panels, grad_b, preferred_element_type=f32).reshape(16, 2, 24, 512)
    keep, send = sort(partial_value[:, 0], partial_value[:, 1])
    keep += lax.ppermute(send.astype(bf16), "c", SWAP).astype(f32)
    projected = collect(keep.astype(bf16), ("x", "y")).astype(bf16)
    projected, moments = lax.optimization_barrier((projected, moments))

    rotated = with_basis(rotate_kernel, projected, basis, (32, 24, 256))
    rotated = collect(rotated.reshape(16, 2, 24, 256), B)
    direction = (adam(moments[0], moments[1], rotated)[2]).astype(bf16)
    direction = spread(direction, B, 16).reshape(32, 24, 256)
    returned = with_basis(back_kernel, direction, basis, (16, 24, 512))
    half = lax.all_to_all(returned, ("x", "y"), 0, 0, tiled=True)
    rotated = lax.ppermute(rotated, ("x", "y", "z", "h"), TURN)
    keep, send = sort(rotated[0], rotated[1])
    rotated = jnp.concatenate(sort(keep, lax.ppermute(send, "c", SWAP)))
    new_moment, new_variance, _ = adam(moment, variance, rotated)
    half, new_moment, new_variance = lax.optimization_barrier((half, new_moment, new_variance))
    returned = lax.all_gather(half, "c", axis=1, tiled=True).reshape(768, 512)
    unscaled = lax.dot_general(
        panels, returned, (((0,), (0,)), ((), ())), preferred_element_type=f32
    )
    sums = jnp.stack([grad_lanes, lanes(unscaled)])
    sums = jnp.sum(spread(sums, ("x", "c"), 8), axis=0)
    update = scale(spread(sums, ("y", "z", "h"), 64), unscaled)
    return (update, new_moment, new_variance)


def solution(mesh):
    fine = Mesh(mesh.devices.reshape(4, 4, 2, 8, 2), F + B)
    return jax.shard_map(
        body,
        mesh=fine,
        in_specs=(P(F, B), P(B, F), P(B, F), P(B, F), P(B, F)),
        out_specs=(P(F, B), P(B, F), P(B, F)),
        check_vma=False,
    )
```

```python
import jax
import jax.numpy as jnp
from jax import lax
from jax.experimental import pallas as pl
from jax.experimental.pallas import tpu as pltpu
from jax.sharding import Mesh, PartitionSpec as P

beta_first = 0.9
beta_second = 0.95
adam_eps = 1e-08
graft_eps = 1e-06

F = ("x", "y", "c")
B = ("z", "h")
SWAP = [(0, 1), (1, 0)]
TURN = [(16 * i + j, 16 * j + i) for i in range(16) for j in range(16)]
PARTS = 4
f32 = jnp.float32
bf16 = jnp.bfloat16


def scale_kernel(sums_ref, unscaled_ref, update_ref, scaled_ref, done_ref):
    total = jnp.sum(sums_ref[...], axis=0)
    root = jnp.sqrt(jnp.sum(total, axis=1, keepdims=True))
    factor = root[0:1] / (root[1:2] + graft_eps)
    size = scaled_ref.shape[0] // PARTS
    copies = []
    for part in range(PARTS):
        rows = pl.ds(part * size, size)
        scaled_ref[rows] = unscaled_ref[rows] * factor
        copies.append(
            pltpu.make_async_copy(scaled_ref.at[rows], update_ref.at[rows], done_ref.at[part])
        )
        copies[-1].start()
    for copy in copies:
        copy.wait()


def scale(sums, unscaled):
    return pl.pallas_call(
        scale_kernel,
        in_specs=[pl.BlockSpec(memory_space=pltpu.VMEM)] * 2,
        out_specs=pl.BlockSpec(memory_space=pl.ANY),
        out_shape=jax.ShapeDtypeStruct(unscaled.shape, f32),
        scratch_shapes=[
            pltpu.VMEM(unscaled.shape, f32),
            pltpu.SemaphoreType.DMA((PARTS,)),
        ],
        compiler_params=pltpu.CompilerParams(vmem_limit_bytes=16 * 2**20),
        cost_estimate=pl.CostEstimate(
            flops=unscaled.size, bytes_accessed=8 * unscaled.size, transcendentals=0
        ),
    )(sums, unscaled)


def lanes(values):
    return jnp.sum(jnp.sum(values * values, axis=0).reshape(-1, 128), axis=0)


def adam(moment, variance, rotated):
    new_moment = beta_first * moment + (1.0 - beta_first) * rotated
    new_variance = beta_second * variance + (1.0 - beta_second) * rotated * rotated
    return new_moment, new_variance, new_moment / (jnp.sqrt(new_variance) + adam_eps)


def spread(block, axes, count):
    copies = jnp.broadcast_to(block[None], (count,) + block.shape)
    return lax.all_to_all(copies, axes, 0, 0, tiled=True)


def collect(parts, axes):
    got = lax.all_to_all(parts, axes, 0, 0, tiled=True)
    terms = [got[i].astype(f32) for i in range(got.shape[0])]
    while len(terms) > 1:
        terms = [a + b for a, b in zip(terms[::2], terms[1::2])]
    return terms[0]


def body(gradient, left_basis, right_basis, moment, variance):
    first = lax.axis_index("c") == 0

    def sort(mine, theirs):
        return jnp.where(first, mine, theirs), jnp.where(first, theirs, mine)

    basis = lax.all_gather(right_basis, F)

    moments = jnp.stack([moment, variance])
    keep, send = sort(moments[:, :24], moments[:, 24:])
    blocks = sort(keep, lax.ppermute(send, "c", SWAP))
    moments = jnp.stack(blocks, axis=1)

    grad_b = gradient.astype(bf16)
    panels = spread(lax.all_gather(left_basis, "h", tiled=True), "z", 8)
    panels, moments, grad_lanes = lax.optimization_barrier((panels, moments, lanes(gradient)))
    moments = lax.ppermute(moments, ("x", "y", "z", "h"), TURN)
    panels = panels.reshape(768, 896)
    partial_value = jnp.dot(panels, grad_b, preferred_element_type=f32).reshape(16, 2, 24, 512)
    keep, send = sort(partial_value[:, 0], partial_value[:, 1])
    keep += lax.ppermute(send.astype(bf16), "c", SWAP).astype(f32)
    projected = collect(keep.astype(bf16), ("x", "y")).astype(bf16)
    projected, moments = lax.optimization_barrier((projected, moments))

    rotated = jnp.einsum("rk,fkn->frn", projected, basis, preferred_element_type=f32)
    rotated = collect(rotated.astype(bf16).reshape(16, 2, 24, 256), B)
    direction = (adam(moments[0], moments[1], rotated)[2]).astype(bf16)
    direction = spread(direction, B, 16).reshape(32, 24, 256)
    returned = lax.dot_general(
        direction, basis, (((0, 2), (0, 2)), ((), ())), preferred_element_type=f32
    )

    half = spread(returned.astype(bf16), ("x", "y"), 16)
    keep, send = sort(rotated[0], rotated[1])
    rotated = jnp.concatenate(sort(keep, lax.ppermute(send, "c", SWAP)))
    half, rotated = lax.optimization_barrier((half, rotated))
    returned = lax.all_gather(half, "c", axis=1, tiled=True).reshape(768, 512)
    unscaled = lax.dot_general(
        panels, returned, (((0,), (0,)), ((), ())), preferred_element_type=f32
    )
    sums = jnp.stack([grad_lanes, lanes(unscaled)])
    sums = jnp.sum(spread(sums, ("x", "c"), 8), axis=0)
    sums, rotated = lax.optimization_barrier((spread(sums, ("y", "z", "h"), 64), rotated))
    rotated = lax.ppermute(rotated, ("x", "y", "z", "h"), TURN)
    update = scale(sums, unscaled)
    new_moment, new_variance, _ = adam(moment, variance, rotated)
    return (update, new_moment, new_variance)


def solution(mesh):
    fine = Mesh(mesh.devices.reshape(4, 4, 2, 8, 2), F + B)
    return jax.shard_map(
        body,
        mesh=fine,
        in_specs=(P(F, B), P(B, F), P(B, F), P(B, F), P(B, F)),
        out_specs=(P(F, B), P(B, F), P(B, F)),
        check_vma=False,
    )
```

```python
import jax
import jax.numpy as jnp
from jax import lax
from jax.experimental import pallas as pl
from jax.experimental.pallas import tpu as pltpu
from jax.sharding import Mesh, PartitionSpec as P

beta_first = 0.9
beta_second = 0.95
adam_eps = 1e-08
graft_eps = 1e-06

F = ("x", "y", "c")
B = ("z", "h")
SWAP = [(0, 1), (1, 0)]
TURN = [(16 * i + j, 16 * j + i) for i in range(16) for j in range(16)]
PARTS = 4
f32 = jnp.float32
bf16 = jnp.bfloat16


def scale_kernel(sums_ref, unscaled_ref, update_ref, scaled_ref, done_ref):
    total = jnp.sum(sums_ref[...], axis=0)
    root = jnp.sqrt(jnp.sum(total, axis=1, keepdims=True))
    factor = root[0:1] / (root[1:2] + graft_eps)
    size = scaled_ref.shape[0] // PARTS
    copies = []
    for part in range(PARTS):
        rows = pl.ds(part * size, size)
        scaled_ref[rows] = unscaled_ref[rows] * factor
        copies.append(
            pltpu.make_async_copy(scaled_ref.at[rows], update_ref.at[rows], done_ref.at[part])
        )
        copies[-1].start()
    for copy in copies:
        copy.wait()


def scale(sums, unscaled):
    return pl.pallas_call(
        scale_kernel,
        in_specs=[pl.BlockSpec(memory_space=pltpu.VMEM)] * 2,
        out_specs=pl.BlockSpec(memory_space=pl.ANY),
        out_shape=jax.ShapeDtypeStruct(unscaled.shape, f32),
        scratch_shapes=[
            pltpu.VMEM(unscaled.shape, f32),
            pltpu.SemaphoreType.DMA((PARTS,)),
        ],
        compiler_params=pltpu.CompilerParams(vmem_limit_bytes=16 * 2**20),
        cost_estimate=pl.CostEstimate(
            flops=unscaled.size, bytes_accessed=8 * unscaled.size, transcendentals=0
        ),
    )(sums, unscaled)


def lanes(values):
    return jnp.sum(jnp.sum(values * values, axis=0).reshape(-1, 128), axis=0)


def adam(moment, variance, rotated):
    new_moment = beta_first * moment + (1.0 - beta_first) * rotated
    new_variance = beta_second * variance + (1.0 - beta_second) * rotated * rotated
    return new_moment, new_variance, new_moment / (jnp.sqrt(new_variance) + adam_eps)


def spread(block, axes, count):
    copies = jnp.broadcast_to(block[None], (count,) + block.shape)
    return lax.all_to_all(copies, axes, 0, 0, tiled=True)


def collect(parts, axes):
    got = lax.all_to_all(parts, axes, 0, 0, tiled=True)
    terms = [got[i].astype(f32) for i in range(got.shape[0])]
    while len(terms) > 1:
        terms = [a + b for a, b in zip(terms[::2], terms[1::2])]
    return terms[0]


def body(gradient, left_basis, right_basis, moment, variance):
    first = lax.axis_index("c") == 0

    def sort(mine, theirs):
        return jnp.where(first, mine, theirs), jnp.where(first, theirs, mine)

    basis = lax.all_gather(right_basis, F)

    moments = jnp.stack([moment, variance])
    keep, send = sort(moments[:, :24], moments[:, 24:])
    blocks = sort(keep, lax.ppermute(send, "c", SWAP))
    moments = jnp.stack(blocks, axis=1)

    grad_b = gradient.astype(bf16)
    panels = spread(lax.all_gather(left_basis, "h", tiled=True), "z", 8)
    panels, moments, grad_lanes = lax.optimization_barrier((panels, moments, lanes(gradient)))
    moments = lax.ppermute(moments, ("x", "y", "z", "h"), TURN)
    panels = panels.reshape(768, 896)
    partial_value = jnp.dot(panels, grad_b, preferred_element_type=f32).reshape(16, 2, 24, 512)
    keep, send = sort(partial_value[:, 0], partial_value[:, 1])
    keep += lax.ppermute(send.astype(bf16), "c", SWAP).astype(f32)
    projected = collect(keep.astype(bf16), ("x", "y")).astype(bf16)
    projected, moments = lax.optimization_barrier((projected, moments))

    rotated = jnp.einsum("rk,fkn->frn", projected, basis, preferred_element_type=f32)
    rotated = collect(rotated.astype(bf16).reshape(16, 2, 24, 256), B)
    direction = (adam(moments[0], moments[1], rotated)[2]).astype(bf16)
    direction = spread(direction, B, 16).reshape(32, 24, 256)
    returned = lax.dot_general(
        direction, basis, (((0, 2), (0, 2)), ((), ())), preferred_element_type=f32
    )

    returned, rotated = lax.optimization_barrier((returned.astype(bf16), rotated))
    half = spread(returned, ("x", "y"), 16)
    keep, send = sort(rotated[0], rotated[1])
    rotated = jnp.concatenate(sort(keep, lax.ppermute(send, "c", SWAP)))
    rotated = lax.ppermute(rotated, ("x", "y", "z", "h"), TURN)
    new_moment, new_variance, _ = adam(moment, variance, rotated)
    returned = lax.all_gather(half, "c", axis=1, tiled=True).reshape(768, 512)
    unscaled = lax.dot_general(
        panels, returned, (((0,), (0,)), ((), ())), preferred_element_type=f32
    )
    sums = jnp.stack([grad_lanes, lanes(unscaled)])
    sums, new_moment, new_variance = lax.optimization_barrier((sums, new_moment, new_variance))
    sums = jnp.sum(spread(sums, ("x", "c"), 8), axis=0)
    update = scale(spread(sums, ("y", "z", "h"), 64), unscaled)
    return (update, new_moment, new_variance)


def solution(mesh):
    fine = Mesh(mesh.devices.reshape(4, 4, 2, 8, 2), F + B)
    return jax.shard_map(
        body,
        mesh=fine,
        in_specs=(P(F, B), P(B, F), P(B, F), P(B, F), P(B, F)),
        out_specs=(P(F, B), P(B, F), P(B, F)),
        check_vma=False,
    )
```

```python
import jax
import jax.numpy as jnp
from jax import lax
from jax.experimental import pallas as pl
from jax.experimental.pallas import tpu as pltpu
from jax.sharding import Mesh, PartitionSpec as P

beta_first = 0.9
beta_second = 0.95
adam_eps = 1e-08
graft_eps = 1e-06

F = ("x", "y", "c")
B = ("z", "h")
SWAP = [(0, 1), (1, 0)]
TURN = [(16 * i + j, 16 * j + i) for i in range(16) for j in range(16)]
PARTS = 4
PIECES = 16
AHEAD = 6
f32 = jnp.float32
bf16 = jnp.bfloat16


def back_kernel(direction_ref, basis_ref, out_ref, held_ref, landed_ref):
    size = held_ref.shape[0] // PIECES
    copies = []
    for piece in range(PIECES):
        blocks = pl.ds(piece * size, size)
        copies.append(
            pltpu.make_async_copy(basis_ref.at[blocks], held_ref.at[blocks], landed_ref.at[piece])
        )
    for copy in copies[:AHEAD]:
        copy.start()
    total = jnp.zeros(out_ref.shape[1:], f32)
    for piece, copy in enumerate(copies):
        copy.wait()
        if piece + AHEAD < PIECES:
            copies[piece + AHEAD].start()
        for block in range(piece * size, (piece + 1) * size):
            total += lax.dot_general(
                direction_ref[block],
                held_ref[block],
                (((1,), (1,)), ((), ())),
                preferred_element_type=f32,
            )
    total = total.astype(bf16)
    for target in range(out_ref.shape[0]):
        out_ref[target] = total


def rotate_back(direction, basis):
    return pl.pallas_call(
        back_kernel,
        in_specs=[pl.BlockSpec(memory_space=pltpu.VMEM), pl.BlockSpec(memory_space=pl.ANY)],
        out_specs=pl.BlockSpec(memory_space=pltpu.VMEM),
        out_shape=jax.ShapeDtypeStruct((16, 24, 512), bf16),
        scratch_shapes=[pltpu.VMEM(basis.shape, bf16), pltpu.SemaphoreType.DMA((PIECES,))],
        compiler_params=pltpu.CompilerParams(vmem_limit_bytes=57 * 2**20),
        cost_estimate=pl.CostEstimate(
            flops=48 * basis.size, bytes_accessed=2 * basis.size, transcendentals=0
        ),
    )(direction, basis)


def scale_kernel(sums_ref, unscaled_ref, update_ref, scaled_ref, done_ref):
    total = jnp.sum(sums_ref[...], axis=0)
    root = jnp.sqrt(jnp.sum(total, axis=1, keepdims=True))
    factor = root[0:1] / (root[1:2] + graft_eps)
    size = scaled_ref.shape[0] // PARTS
    copies = []
    for part in range(PARTS):
        rows = pl.ds(part * size, size)
        scaled_ref[rows] = unscaled_ref[rows] * factor
        copies.append(
            pltpu.make_async_copy(scaled_ref.at[rows], update_ref.at[rows], done_ref.at[part])
        )
        copies[-1].start()
    for copy in copies:
        copy.wait()


def scale(sums, unscaled):
    return pl.pallas_call(
        scale_kernel,
        in_specs=[pl.BlockSpec(memory_space=pltpu.VMEM)] * 2,
        out_specs=pl.BlockSpec(memory_space=pl.ANY),
        out_shape=jax.ShapeDtypeStruct(unscaled.shape, f32),
        scratch_shapes=[
            pltpu.VMEM(unscaled.shape, f32),
            pltpu.SemaphoreType.DMA((PARTS,)),
        ],
        compiler_params=pltpu.CompilerParams(vmem_limit_bytes=16 * 2**20),
        cost_estimate=pl.CostEstimate(
            flops=unscaled.size, bytes_accessed=8 * unscaled.size, transcendentals=0
        ),
    )(sums, unscaled)


def lanes(values):
    return jnp.sum(jnp.sum(values * values, axis=0).reshape(-1, 128), axis=0)


def adam(moment, variance, rotated):
    new_moment = beta_first * moment + (1.0 - beta_first) * rotated
    new_variance = beta_second * variance + (1.0 - beta_second) * rotated * rotated
    return new_moment, new_variance, new_moment / (jnp.sqrt(new_variance) + adam_eps)


def spread(block, axes, count):
    copies = jnp.broadcast_to(block[None], (count,) + block.shape)
    return lax.all_to_all(copies, axes, 0, 0, tiled=True)


def collect(parts, axes):
    got = lax.all_to_all(parts, axes, 0, 0, tiled=True)
    terms = [got[i].astype(f32) for i in range(got.shape[0])]
    while len(terms) > 1:
        terms = [a + b for a, b in zip(terms[::2], terms[1::2])]
    return terms[0]


def body(gradient, left_basis, right_basis, moment, variance):
    first = lax.axis_index("c") == 0

    def sort(mine, theirs):
        return jnp.where(first, mine, theirs), jnp.where(first, theirs, mine)

    basis = lax.all_gather(right_basis, F)

    moments = jnp.stack([moment, variance])
    keep, send = sort(moments[:, :24], moments[:, 24:])
    blocks = sort(keep, lax.ppermute(send, "c", SWAP))
    moments = jnp.stack(blocks, axis=1)

    grad_b = gradient.astype(bf16)
    panels = spread(lax.all_gather(left_basis, "h", tiled=True), "z", 8)
    panels, moments, grad_lanes = lax.optimization_barrier((panels, moments, lanes(gradient)))
    moments = lax.ppermute(moments, ("x", "y", "z", "h"), TURN)
    panels = panels.reshape(768, 896)
    partial_value = jnp.dot(panels, grad_b, preferred_element_type=f32).reshape(16, 2, 24, 512)
    keep, send = sort(partial_value[:, 0], partial_value[:, 1])
    keep += lax.ppermute(send.astype(bf16), "c", SWAP).astype(f32)
    projected = collect(keep.astype(bf16), ("x", "y")).astype(bf16)
    projected, moments = lax.optimization_barrier((projected, moments))

    rotated = jnp.einsum("rk,fkn->frn", projected, basis, preferred_element_type=f32)
    rotated = collect(rotated.astype(bf16).reshape(16, 2, 24, 256), B)
    direction = (adam(moments[0], moments[1], rotated)[2]).astype(bf16)
    direction = spread(direction, B, 16).reshape(32, 24, 256)
    half = lax.all_to_all(rotate_back(direction, basis), ("x", "y"), 0, 0, tiled=True)
    rotated = lax.ppermute(rotated, ("x", "y", "z", "h"), TURN)
    keep, send = sort(rotated[0], rotated[1])
    rotated = jnp.concatenate(sort(keep, lax.ppermute(send, "c", SWAP)))
    new_moment, new_variance, _ = adam(moment, variance, rotated)
    half, new_moment, new_variance = lax.optimization_barrier((half, new_moment, new_variance))
    returned = lax.all_gather(half, "c", axis=1, tiled=True).reshape(768, 512)
    unscaled = lax.dot_general(
        panels, returned, (((0,), (0,)), ((), ())), preferred_element_type=f32
    )
    sums = jnp.stack([grad_lanes, lanes(unscaled)])
    sums = jnp.sum(spread(sums, ("x", "c"), 8), axis=0)
    update = scale(spread(sums, ("y", "z", "h"), 64), unscaled)
    return (update, new_moment, new_variance)


def solution(mesh):
    fine = Mesh(mesh.devices.reshape(4, 4, 2, 8, 2), F + B)
    return jax.shard_map(
        body,
        mesh=fine,
        in_specs=(P(F, B), P(B, F), P(B, F), P(B, F), P(B, F)),
        out_specs=(P(F, B), P(B, F), P(B, F)),
        check_vma=False,
    )
```

```python
import jax
import jax.numpy as jnp
from jax import lax
from jax.experimental import pallas as pl
from jax.experimental.pallas import tpu as pltpu
from jax.sharding import Mesh, PartitionSpec as P

beta_first = 0.9
beta_second = 0.95
adam_eps = 1e-08
graft_eps = 1e-06

F = ("x", "y", "c")
B = ("z", "h")
SWAP = [(0, 1), (1, 0)]
TURN = [(16 * i + j, 16 * j + i) for i in range(16) for j in range(16)]
PARTS = 4
f32 = jnp.float32
bf16 = jnp.bfloat16


def scale_kernel(sums_ref, unscaled_ref, update_ref, scaled_ref, done_ref):
    total = jnp.sum(sums_ref[...], axis=0)
    root = jnp.sqrt(jnp.sum(total, axis=1, keepdims=True))
    factor = root[0:1] / (root[1:2] + graft_eps)
    size = scaled_ref.shape[0] // PARTS
    copies = []
    for part in range(PARTS):
        rows = pl.ds(part * size, size)
        scaled_ref[rows] = unscaled_ref[rows] * factor
        copies.append(
            pltpu.make_async_copy(scaled_ref.at[rows], update_ref.at[rows], done_ref.at[part])
        )
        copies[-1].start()
    for copy in copies:
        copy.wait()


def scale(sums, unscaled):
    return pl.pallas_call(
        scale_kernel,
        in_specs=[pl.BlockSpec(memory_space=pltpu.VMEM)] * 2,
        out_specs=pl.BlockSpec(memory_space=pl.ANY),
        out_shape=jax.ShapeDtypeStruct(unscaled.shape, f32),
        scratch_shapes=[
            pltpu.VMEM(unscaled.shape, f32),
            pltpu.SemaphoreType.DMA((PARTS,)),
        ],
        compiler_params=pltpu.CompilerParams(vmem_limit_bytes=16 * 2**20),
        cost_estimate=pl.CostEstimate(
            flops=unscaled.size, bytes_accessed=8 * unscaled.size, transcendentals=0
        ),
    )(sums, unscaled)


def lanes(values):
    return jnp.sum(jnp.sum(values * values, axis=0).reshape(-1, 128), axis=0)


def adam(moment, variance, rotated):
    new_moment = beta_first * moment + (1.0 - beta_first) * rotated
    new_variance = beta_second * variance + (1.0 - beta_second) * rotated * rotated
    return new_moment, new_variance, new_moment / (jnp.sqrt(new_variance) + adam_eps)


def spread(block, axes, count):
    copies = jnp.broadcast_to(block[None], (count,) + block.shape)
    return lax.all_to_all(copies, axes, 0, 0, tiled=True)


def collect(parts, axes):
    got = lax.all_to_all(parts, axes, 0, 0, tiled=True)
    terms = [got[i].astype(f32) for i in range(got.shape[0])]
    while len(terms) > 1:
        terms = [a + b for a, b in zip(terms[::2], terms[1::2])]
    return terms[0]


def body(gradient, left_basis, right_basis, moment, variance):
    first = lax.axis_index("c") == 0

    def sort(mine, theirs):
        return jnp.where(first, mine, theirs), jnp.where(first, theirs, mine)

    basis = lax.all_gather(right_basis, F)

    moments = jnp.stack([moment, variance])
    keep, send = sort(moments[:, :24], moments[:, 24:])
    blocks = sort(keep, lax.ppermute(send, "c", SWAP))
    moments = jnp.stack(blocks, axis=1)

    grad_b = gradient.astype(bf16)
    panels = spread(lax.all_gather(left_basis, "h", tiled=True), "z", 8)
    panels, moments, grad_lanes = lax.optimization_barrier((panels, moments, lanes(gradient)))
    moments = lax.ppermute(moments, ("x", "y", "z", "h"), TURN)
    panels = panels.reshape(768, 896)
    partial_value = jnp.dot(panels, grad_b, preferred_element_type=f32).reshape(16, 2, 24, 512)
    keep, send = sort(partial_value[:, 0], partial_value[:, 1])
    keep += lax.ppermute(send.astype(bf16), "c", SWAP).astype(f32)
    projected = collect(keep.astype(bf16), ("x", "y")).astype(bf16)
    projected, moments = lax.optimization_barrier((projected, moments))

    rotated = jnp.einsum("rk,fkn->frn", projected, basis, preferred_element_type=f32)
    rotated = collect(rotated.astype(bf16).reshape(16, 2, 24, 256), B)
    direction = (adam(moments[0], moments[1], rotated)[2]).astype(bf16)
    direction = spread(direction, B, 16).reshape(32, 24, 256)
    returned = lax.dot_general(
        direction, basis, (((0, 2), (0, 2)), ((), ())), preferred_element_type=f32
    )

    returned, rotated = lax.optimization_barrier((returned.astype(bf16), rotated))
    half = spread(returned, ("x", "y"), 16)
    rotated = lax.ppermute(rotated, ("x", "y", "z", "h"), TURN)
    keep, send = sort(rotated[0], rotated[1])
    rotated = jnp.concatenate(sort(keep, lax.ppermute(send, "c", SWAP)))
    new_moment, new_variance, _ = adam(moment, variance, rotated)
    half, new_moment, new_variance = lax.optimization_barrier((half, new_moment, new_variance))
    returned = lax.all_gather(half, "c", axis=1, tiled=True).reshape(768, 512)
    unscaled = lax.dot_general(
        panels, returned, (((0,), (0,)), ((), ())), preferred_element_type=f32
    )
    sums = jnp.stack([grad_lanes, lanes(unscaled)])
    sums = jnp.sum(spread(sums, ("x", "c"), 8), axis=0)
    update = scale(spread(sums, ("y", "z", "h"), 64), unscaled)
    return (update, new_moment, new_variance)


def solution(mesh):
    fine = Mesh(mesh.devices.reshape(4, 4, 2, 8, 2), F + B)
    return jax.shard_map(
        body,
        mesh=fine,
        in_specs=(P(F, B), P(B, F), P(B, F), P(B, F), P(B, F)),
        out_specs=(P(F, B), P(B, F), P(B, F)),
        check_vma=False,
    )
```
